32 devices in a mesh: dp: 4 (over z), expert: 4 (over x, core), tensor: 2 (over y).
Axes of the slice: x: 2, y: 2, z: 4, core: 2. Of those that a mesh axis runs over, the one named last changes fastest.
Arguments:
- tokens: bfloat16 [128, 4096], P(('dp', 'expert')), may hold values from -6 to 6
- grad_out: bfloat16 [128, 4096], P(('dp', 'expert')), may hold values from -6 to 6
- slot_token: int32 [16, 32], P(('dp', 'expert')), may hold values from 0 to 31, as said below
- slot_count: int32 [16], P(('dp', 'expert')), may hold values from 16 to 32, as said below
- slot_gate: float32 [16, 32], P(('dp', 'expert')), may hold values from 0.05 to 1
- w_gate: bfloat16 [4, 4096, 768], P('expert', 'dp', 'tensor'), may hold values from -0.09375 to 0.09375
- w_up: bfloat16 [4, 4096, 768], P('expert', 'dp', 'tensor'), may hold values from -0.09375 to 0.09375
- w_down: bfloat16 [4, 768, 4096], P('expert', 'tensor', 'dp'), may hold values from -0.21875 to 0.21875
Outputs:
- grad_tokens: bfloat16 [128, 4096], P(('dp', 'expert'))
- grad_gate: float32 [16, 32], P(('dp', 'expert'))
- grad_w_gate: bfloat16 [4, 4096, 768], P('expert', 'dp', 'tensor')
- grad_w_up: bfloat16 [4, 4096, 768], P('expert', 'dp', 'tensor')
- grad_w_down: bfloat16 [4, 768, 4096], P('expert', 'tensor', 'dp')
The draws below stay inside these ranges and needn't reach their ends.
Inputs may be any that keep to these rules, and one draw needn't show every extreme that they name: `slot_token`: the 32 entries of one list are distinct, and a token lies in at most 4 lists of its index of dp. Slots from slot_count[r] on are unused.
All inputs are finite; a program needn't handle non-finite values.
Results may differ from the reference program's by a relative error of at most 0.015.
Values may be sent and summed in bfloat16 or wider, within the bound.
A program may use at most 64 MiB of HBM per device.

```python
import jax
import jax.numpy as jnp
from jax import lax

D = 4096
F = 768
TOK_DEV = 8
FLIGHT = 4
ROWS_GRP = 32
CAP = 32
GROUPS = 16
BLOCK = 1024
TOKENS = 128
N_DP = 4


def draw_slot_token(key, part):
    key = jax.random.fold_in(key, 11)
    group_keys = jax.random.split(key, GROUPS // FLIGHT)
    permuted = jax.vmap(lambda single: jax.random.permutation(single, ROWS_GRP))(group_keys)
    position = (jnp.arange(FLIGHT)[:, None] * TOK_DEV + jnp.arange(CAP)[None, :]) % ROWS_GRP
    return permuted[:, position].reshape(GROUPS, CAP).astype(jnp.int32)


def draw_slot_count(key, part):
    key = jax.random.fold_in(key, 12)
    count_key, pick_key = jax.random.split(key, 2)
    counts = jax.random.randint(count_key, (GROUPS,), CAP // 2, CAP + 1)
    chosen = jax.random.randint(pick_key, (), 0, GROUPS)
    return jnp.where(jnp.arange(GROUPS) == chosen, CAP, counts).astype(jnp.int32)


def levels(stream_key, dims, shards, low, top_value):
    def one(dim, parts):
        steps = jax.random.uniform(jax.random.fold_in(jax.random.fold_in(stream_key, 6), dim), (parts,), jnp.float32, low / len(shards), top_value / len(shards))
        return jnp.repeat(jnp.exp(steps), dims[dim] // parts).reshape((-1,) + (1,) * (len(dims) - dim - 1))

    factor_of = one(*shards[0])
    for cut in shards[1:]:
        factor_of = factor_of * one(*cut)
    return factor_of


def scatter_about(rng, dims, deviation, bound, cuts=(), kind=jnp.bfloat16):
    level = levels(rng, dims, cuts, -0.22, 0.18) if cuts else 1.0
    values = jax.random.normal(rng, dims, jnp.float32) * deviation * level
    return jnp.minimum(jnp.maximum(values, -bound), bound).astype(kind)


def setup_inputs(seed: int = 0) -> dict:
    key_list = jax.random.split(jax.random.key(seed), 9)
    return {
        "tokens": scatter_about(key_list[0], (TOKENS, D), 1.0, 6.0, ((0, 16),)),
        "grad_out": scatter_about(key_list[1], (TOKENS, D), 0.5, 6.0, ((0, 16),)),
        "slot_token": draw_slot_token(jax.random.fold_in(key_list[8], 71), 0),
        "slot_count": draw_slot_count(jax.random.fold_in(key_list[8], 71), 0),
        "slot_gate": jnp.clip(0.05 + 0.95 * jax.random.uniform(key_list[4], (GROUPS, CAP), jnp.float32) ** levels(key_list[4], (GROUPS, CAP), ((0, 16),), -0.2, 0.2), 0.05, 1.0),
        "w_gate": scatter_about(key_list[5], (FLIGHT, D, F), D ** -0.5, 0.09375, ((0, 4), (1, 4), (2, 2))),
        "w_up": scatter_about(key_list[6], (FLIGHT, D, F), D ** -0.5, 0.09375, ((0, 4), (1, 4), (2, 2))),
        "w_down": scatter_about(key_list[7], (FLIGHT, F, D), F ** -0.5, 0.21875, ((0, 4), (1, 2), (2, 4))),
    }


def swish_slope(pre_act):
    sigmoid_value = jax.nn.sigmoid(pre_act)
    return sigmoid_value * (1.0 + pre_act * (1.0 - sigmoid_value))


def blockwise(rows, weight, block_width):
    row_total = rows.shape[0]
    blocks = rows.reshape(row_total, -1, block_width)
    weight_blocks = weight.reshape(-1, block_width, weight.shape[1])
    block_parts = jnp.einsum("rnd,ndf->nrf", blocks, weight_blocks)
    rounded = lax.optimization_barrier(block_parts.astype(jnp.bfloat16))
    return jnp.sum(rounded.astype(jnp.float32), axis=0)


def reference(tokens, grad_out, slot_token, slot_count, slot_gate, w_gate, w_up, w_down):
    is_live = jnp.arange(CAP)[None, :] < slot_count[:, None]
    gate_live = jnp.where(is_live, slot_gate, jnp.float32(0.0)).astype(jnp.float32)
    offsets = ((jnp.arange(GROUPS) // FLIGHT) * ROWS_GRP).astype(jnp.int32)
    global_index = (slot_token + offsets[:, None]).astype(jnp.int32)
    index_by = global_index.reshape(N_DP, FLIGHT, CAP).transpose(1, 0, 2)
    gates_by = gate_live.reshape(N_DP, FLIGHT, CAP).transpose(1, 0, 2)
    live_by = is_live.reshape(N_DP, FLIGHT, CAP).transpose(1, 0, 2)

    def one_expert(running, inputs):
        slot_index, gate_rows, live_rows, gate_weight, up_weight, down_weight = inputs
        flat_index = slot_index.reshape(-1)
        rows_x = tokens[flat_index]
        rows_dy = grad_out[flat_index]
        wide_x = rows_x.astype(jnp.float32)
        wide_dy = rows_dy.astype(jnp.float32)
        pre_gate = blockwise(wide_x, gate_weight.astype(jnp.float32), BLOCK)
        pre_up = blockwise(wide_x, up_weight.astype(jnp.float32), BLOCK)
        back_grad = blockwise(wide_dy, down_weight.T.astype(jnp.float32), BLOCK)
        hidden = jax.nn.silu(pre_gate) * pre_up
        flat_gate = gate_rows.reshape(-1)
        flat_live = live_rows.reshape(-1)
        gate_grad = jnp.where(flat_live, jnp.sum(hidden * back_grad, axis=1), jnp.float32(0.0))
        d_hidden = flat_gate[:, None] * back_grad
        d_up = (d_hidden * jax.nn.silu(pre_gate)).astype(jnp.bfloat16)
        d_gate = (d_hidden * pre_up * swish_slope(pre_gate)).astype(jnp.bfloat16)
        scaled = (flat_gate[:, None] * hidden).astype(jnp.bfloat16)
        grad_wg = jnp.dot(rows_x.T, d_gate, preferred_element_type=jnp.float32).astype(jnp.bfloat16)
        grad_wu = jnp.dot(rows_x.T, d_up, preferred_element_type=jnp.float32).astype(jnp.bfloat16)
        grad_wd = jnp.dot(scaled.T, rows_dy, preferred_element_type=jnp.float32).astype(jnp.bfloat16)
        d_rows = (jnp.dot(d_gate, gate_weight.T, preferred_element_type=jnp.float32)
                  + jnp.dot(d_up, up_weight.T, preferred_element_type=jnp.float32)).astype(jnp.bfloat16)
        running = running.at[flat_index].add(d_rows.astype(jnp.float32))
        return running, (gate_grad.reshape(N_DP, CAP), grad_wg, grad_wu, grad_wd)

    start_grad = jnp.zeros((TOKENS, D), jnp.float32)
    total, stacked = lax.scan(one_expert, start_grad, (index_by, gates_by, live_by, w_gate, w_up, w_down))
    gate_grads, grad_w_gate, grad_w_up, grad_w_down = stacked
    grad_gate = gate_grads.transpose(1, 0, 2).reshape(GROUPS, CAP)
    return total.astype(jnp.bfloat16), grad_gate, grad_w_gate, grad_w_up, grad_w_down
```

```python
import functools

import jax
import jax.numpy as jnp
from jax import lax
from jax.experimental import pallas as pl
from jax.experimental.pallas import tpu as pltpu
from jax.sharding import PartitionSpec as P

MESH = pl.DeviceIdType.MESH
F32 = jnp.float32
BF16 = jnp.bfloat16


def nn(a, b):
    return lax.dot_general(a, b, (((1,), (0,)), ((), ())), preferred_element_type=F32)


def nt(a, b):
    return lax.dot_general(a, b, (((1,), (1,)), ((), ())), preferred_element_type=F32)


def kernel(
    n, ex, tn,
    x_ref, dy_ref, slot_ref, count_ref, gate_ref, wg_hbm, wu_hbm, wd_hbm,
    gt_ref, gg_ref, gwg_hbm, gwu_hbm, gwd_hbm,
    wg, wu, wd, owg, owu, owd, src, full, xs, ys, xt, ps, pr, dgu, dsc,
    dsend, drecv, esend, erecv, gsend, grecv,
    w_sem, o_sem, a1s, a1r, a2s, a2r, bs, br, cs, cr, ss, sr, ds_, dr, es, er, gs, gr,
):
    d = lax.axis_index("dp")
    e = lax.axis_index("expert")
    t = lax.axis_index("tensor")
    tl = x_ref.shape[0]
    bw = xs.shape[1]
    hid = wg.shape[1]
    rows = ex * tl
    half = n // tn
    cap = slot_ref.shape[1]
    chunks = a2s.shape[0]
    per = n // chunks

    def remote(s, r, ssem, rsem, dd, ee, tt):
        return pltpu.make_async_remote_copy(
            src_ref=s, dst_ref=r, send_sem=ssem, recv_sem=rsem,
            device_id=(dd, ee, tt), device_id_type=MESH,
        )

    barrier = pltpu.get_barrier_semaphore()
    greeted = 0
    for dd in range(n):
        for ee in range(ex):
            for tt in range(tn):
                if (dd and ee) or not (dd or ee or tt):
                    continue
                pl.semaphore_signal(
                    barrier, inc=1,
                    device_id=(lax.rem(d + dd, n), lax.rem(e + ee, ex), lax.rem(t + tt, tn)),
                    device_id_type=MESH,
                )
                greeted += 1

    loads = [
        pltpu.make_async_copy(wg_hbm.at[0], wg, w_sem.at[0]),
        pltpu.make_async_copy(wu_hbm.at[0], wu, w_sem.at[1]),
        pltpu.make_async_copy(wd_hbm.at[0], wd, w_sem.at[2]),
    ]
    for load in loads:
        load.start()

    for b in range(n):
        cols = slice(b * bw, (b + 1) * bw)
        both = jnp.concatenate([x_ref[:, cols].astype(F32), dy_ref[:, cols].astype(F32)], axis=0)
        src[b] = both.astype(BF16)
    full[d, e] = src[d]
    gsend[...] = jnp.zeros_like(gsend)

    pl.semaphore_wait(barrier, greeted)

    to_dp = []
    for k in range(1, n):
        p = lax.rem(d + k, n)
        c = remote(src.at[p], full.at[d, e], a1s.at[p], a1r.at[d], p, e, t)
        c.start()
        to_dp.append(c)
    to_expert = []
    for k in range(chunks):
        chunk = lax.rem(d // per + k, chunks)
        for q in range(per):
            g = chunk * per + q
            if per == 1:
                if k:
                    remote(src.at[g], full.at[g, e], a1s.at[g], a1r.at[g], g, e, t).wait_recv()
            else:
                @pl.when(g != d)
                def _():
                    remote(src.at[g], full.at[g, e], a1s.at[g], a1r.at[g], g, e, t).wait_recv()
        span = pl.ds(chunk * per, per)
        for j in range(1, ex):
            p = lax.rem(e + j, ex)
            c = remote(full.at[span, e], full.at[span, e], a2s.at[chunk, p], a2r.at[chunk, e], d, p, t)
            c.start()
            to_expert.append(c)
    for k in range(chunks):
        chunk = lax.rem(d // per + k, chunks)
        span = pl.ds(chunk * per, per)
        for j in range(1, ex):
            p = lax.rem(e + j, ex)
            remote(full.at[span, p], full.at[span, p], a2s.at[chunk, p], a2r.at[chunk, p], d, p, t).wait_recv()
    for c in to_dp:
        c.wait_send()
    for c in to_expert:
        c.wait_send()
    for g in range(n):
        wide = full[g].astype(F32)
        xs[g * rows:(g + 1) * rows, :] = wide[:, :tl].reshape(rows, bw).astype(BF16)
        ys[g * rows:(g + 1) * rows, :] = wide[:, tl:].reshape(rows, bw).astype(BF16)

    to_owner = []
    for i, (act, w, mul) in enumerate(((xs, wg, nn), (xs, wu, nn), (ys, wd, nt))):
        loads[i].wait()
        ps[i] = mul(act[...], w[...]).astype(BF16).reshape(n, rows, hid)
        for k in range(1, n):
            p = lax.rem(d + k, n)
            c = remote(ps.at[i, p], pr.at[i, d], bs.at[i, p], br.at[i, d], p, e, t)
            c.start()
            to_owner.append(c)
    xt[...] = xs[...].T

    iota_slot = lax.broadcasted_iota(jnp.int32, (1, cap), 1)
    live = iota_slot < count_ref[0]
    gate_live = jnp.where(live, gate_ref[...], 0.0)
    holds = lax.broadcasted_iota(jnp.int32, (rows, cap), 0) == slot_ref[...]
    gate_tok = jnp.sum(jnp.where(holds, gate_live, 0.0), axis=1, keepdims=True)

    sums = []
    for i in range(3):
        total = ps[i, d].astype(F32)
        for k in range(1, n):
            p = lax.rem(d + k, n)
            remote(ps.at[i, p], pr.at[i, p], bs.at[i, p], br.at[i, p], p, e, t).wait_recv()
            total = total + pr[i, p].astype(F32)
        sums.append(total)
    pre_gate, pre_up, back = sums
    sig = 1.0 / (1.0 + jnp.exp(-pre_gate))
    silu = pre_gate * sig
    hidden = silu * pre_up
    d_hidden = gate_tok * back
    dgu[d, 0] = (d_hidden * pre_up * (sig * (1.0 + pre_gate * (1.0 - sig)))).astype(BF16)
    dgu[d, 1] = (d_hidden * silu).astype(BF16)
    to_all = []
    for k in range(1, n):
        p = lax.rem(d + k, n)
        c = remote(dgu.at[d], dgu.at[d], cs.at[p], cr.at[d], p, e, t)
        c.start()
        to_all.append(c)
    dsc[d] = (gate_tok * hidden).astype(BF16)
    for k in range(1, n):
        p = lax.rem(d + k, n)
        c = remote(dsc.at[d], dsc.at[d], ss.at[p], sr.at[d], p, e, t)
        c.start()
        to_all.append(c)
    terms = jnp.sum(hidden * back, axis=1, keepdims=True)
    gsend[0:1, 0:cap] = jnp.where(
        live, jnp.sum(jnp.where(holds, terms, 0.0), axis=0, keepdims=True), 0.0
    )
    for k in range(1, tn):
        p = lax.rem(t + k, tn)
        c = remote(gsend, grecv.at[t], gs.at[p], gr.at[t], d, e, p)
        c.start()
        to_all.append(c)

    for k in range(1, n):
        p = lax.rem(d + k, n)
        remote(dgu.at[p], dgu.at[p], cs.at[p], cr.at[p], p, e, t).wait_recv()
    all_gate = dgu[:, 0].reshape(n * rows, hid)
    all_up = dgu[:, 1].reshape(n * rows, hid)
    d_rows = (nt(all_gate, wg[...]) + nt(all_up, wu[...])).reshape(n, ex, tl, bw)
    for ee in range(ex):
        for tt in range(tn):
            part = d_rows[tt * half:(tt + 1) * half, ee].reshape(half * tl, bw)
            dsend[ee * tn + tt] = part.astype(BF16)
    me = e * tn + t
    for ee in range(ex):
        for tt in range(tn):
            if ee or tt:
                pe, pt = lax.rem(e + ee, ex), lax.rem(t + tt, tn)
                c = remote(dsend.at[pe * tn + pt], drecv.at[me], ds_.at[pe * tn + pt], dr.at[me], d, pe, pt)
                c.start()
                to_all.append(c)

    owg[...] = nn(xt[...], all_gate).astype(BF16)
    stores = [pltpu.make_async_copy(owg, gwg_hbm.at[0], o_sem.at[0])]
    stores[0].start()

    total = dsend[me].astype(F32)
    for ee in range(ex):
        for tt in range(tn):
            if ee or tt:
                other = lax.rem(e + ee, ex) * tn + lax.rem(t + tt, tn)
                remote(dsend.at[other], drecv.at[other], ds_.at[other], dr.at[other], d, e, t).wait_recv()
                total = total + drecv[other].astype(F32)
    mine = d // half == t
    for q in range(half):
        part = total[q * tl:(q + 1) * tl]
        esend[q] = jnp.concatenate([part[:, :bw // 2], part[:, bw // 2:]], axis=0).astype(BF16)
        g = t * half + q
        for tt in range(tn):
            here = jnp.logical_and(g == d, t == tt)

            @pl.when(jnp.logical_not(here))
            def _():
                remote(esend.at[q], erecv.at[d], es.at[q, tt], er.at[d], g, e, tt).start()

            @pl.when(here)
            def _():
                erecv[d] = esend[q]

    owu[...] = nn(xt[...], all_up).astype(BF16)
    stores.append(pltpu.make_async_copy(owu, gwu_hbm.at[0], o_sem.at[1]))
    stores[1].start()
    for k in range(1, n):
        p = lax.rem(d + k, n)
        remote(dsc.at[p], dsc.at[p], ss.at[p], sr.at[p], p, e, t).wait_recv()
    owd[...] = nn(dsc[...].reshape(n * rows, hid).T, ys[...]).astype(BF16)
    stores.append(pltpu.make_async_copy(owd, gwd_hbm.at[0], o_sem.at[2]))
    stores[2].start()

    gate_sum = gsend[0:1, 0:cap]
    for k in range(1, tn):
        p = lax.rem(t + k, tn)
        remote(gsend, grecv.at[p], gs.at[p], gr.at[p], d, e, p).wait_recv()
        gate_sum = gate_sum + grecv[p, 0:1, 0:cap]
    gg_ref[...] = gate_sum

    for s in range(n):
        @pl.when(jnp.logical_not(jnp.logical_and(s == d, mine)))
        def _():
            remote(esend.at[0], erecv.at[s], es.at[0, 0], er.at[s], d, e, t).wait_recv()
        wide = erecv[s].astype(F32)
        gt_ref[:, s * bw:s * bw + bw // 2] = wide[:tl].astype(BF16)
        gt_ref[:, s * bw + bw // 2:(s + 1) * bw] = wide[tl:].astype(BF16)

    for c in to_owner + to_all:
        c.wait_send()
    for q in range(half):
        for tt in range(tn):
            @pl.when(jnp.logical_not(jnp.logical_and(t * half + q == d, t == tt)))
            def _():
                remote(esend.at[q], erecv.at[d], es.at[q, tt], er.at[d], d, e, tt).wait_send()
    for c in stores:
        c.wait()


def shards(n, ex, tn, tokens, grad_out, slot_token, slot_count, slot_gate, w_gate, w_up, w_down):
    tl, width = tokens.shape
    bw, hid = w_gate.shape[1:]
    rows = ex * tl
    all_rows = n * rows
    half = n // tn
    chunks = min(n, 4)
    vmem = pl.BlockSpec(memory_space=pltpu.VMEM)
    anywhere = pl.BlockSpec(memory_space=pl.ANY)
    dma = pltpu.SemaphoreType.DMA
    return pl.pallas_call(
        functools.partial(kernel, n, ex, tn),
        out_shape=(
            jax.ShapeDtypeStruct((tl, width), BF16),
            jax.ShapeDtypeStruct(slot_gate.shape, F32),
            jax.ShapeDtypeStruct(w_gate.shape, BF16),
            jax.ShapeDtypeStruct(w_up.shape, BF16),
            jax.ShapeDtypeStruct(w_down.shape, BF16),
        ),
        in_specs=[vmem, vmem, vmem, pl.BlockSpec(memory_space=pltpu.SMEM), vmem]
        + [anywhere] * 3,
        out_specs=(vmem, vmem, anywhere, anywhere, anywhere),
        scratch_shapes=[
            pltpu.VMEM((bw, hid), BF16),
            pltpu.VMEM((bw, hid), BF16),
            pltpu.VMEM((hid, bw), BF16),
            pltpu.VMEM((bw, hid), BF16),
            pltpu.VMEM((bw, hid), BF16),
            pltpu.VMEM((hid, bw), BF16),
            pltpu.VMEM((n, 2 * tl, bw), BF16),
            pltpu.VMEM((n, ex, 2 * tl, bw), BF16),
            pltpu.VMEM((all_rows, bw), BF16),
            pltpu.VMEM((all_rows, bw), BF16),
            pltpu.VMEM((bw, all_rows), BF16),
            pltpu.VMEM((3, n, rows, hid), BF16),
            pltpu.VMEM((3, n, rows, hid), BF16),
            pltpu.VMEM((n, 2, rows, hid), BF16),
            pltpu.VMEM((n, rows, hid), BF16),
            pltpu.VMEM((ex * tn, half * tl, bw), BF16),
            pltpu.VMEM((ex * tn, half * tl, bw), BF16),
            pltpu.VMEM((half, 2 * tl, bw // 2), BF16),
            pltpu.VMEM((n, 2 * tl, bw // 2), BF16),
            pltpu.VMEM((8, 128), F32),
            pltpu.VMEM((tn, 8, 128), F32),
            dma((3,)), dma((3,)),
            dma((n,)), dma((n,)),
            dma((chunks, ex)), dma((chunks, ex)),
            dma((3, n)), dma((3, n)),
            dma((n,)), dma((n,)),
            dma((n,)), dma((n,)),
            dma((ex * tn,)), dma((ex * tn,)),
            dma((half, tn)), dma((n,)),
            dma((tn,)), dma((tn,)),
        ],
        compiler_params=pltpu.CompilerParams(
            collective_id=0, has_side_effects=True, vmem_limit_bytes=48 * 1024 * 1024
        ),
    )(tokens, grad_out, slot_token, slot_count, slot_gate, w_gate, w_up, w_down)


def solution(mesh):
    n, ex, tn = (mesh.shape[a] for a in ("dp", "expert", "tensor"))
    return jax.shard_map(
        functools.partial(shards, n, ex, tn),
        mesh=mesh,
        in_specs=(
            P(("dp", "expert"), None),
            P(("dp", "expert"), None),
            P(("dp", "expert"), None),
            P(("dp", "expert")),
            P(("dp", "expert"), None),
            P("expert", "dp", "tensor"),
            P("expert", "dp", "tensor"),
            P("expert", "tensor", "dp"),
        ),
        out_specs=(
            P(("dp", "expert"), None),
            P(("dp", "expert"), None),
            P("expert", "dp", "tensor"),
            P("expert", "dp", "tensor"),
            P("expert", "tensor", "dp"),
        ),
        check_vma=False,
    )
```

```python
import functools

import jax
import jax.numpy as jnp
from jax import lax
from jax.experimental import pallas as pl
from jax.experimental.pallas import tpu as pltpu
from jax.sharding import PartitionSpec as P

MESH = pl.DeviceIdType.MESH
F32 = jnp.float32
BF16 = jnp.bfloat16


def nn(a, b):
    return lax.dot_general(a, b, (((1,), (0,)), ((), ())), preferred_element_type=F32)


def nt(a, b):
    return lax.dot_general(a, b, (((1,), (1,)), ((), ())), preferred_element_type=F32)


def kernel(
    n, ex, tn,
    x_hbm, dy_hbm, slot_ref, count_ref, gate_ref, wg_hbm, wu_hbm, wd_hbm,
    gt_ref, gg_ref, xt, ys, ag_ref, au_ref, st_ref,
    x_ref, dy_ref, wg, wu, wd, src, full, xs, ps, pr, dgu, dsc,
    dsend, drecv, esend, erecv, gsend, grecv,
    t_sem, w_sem, a1s, a1r, a2s, a2r, bs, br, cs, cr, ss, sr, ds_, dr, es, er, gs, gr,
):
    d = lax.axis_index("dp")
    e = lax.axis_index("expert")
    t = lax.axis_index("tensor")
    tl = x_ref.shape[0]
    bw = xs.shape[1]
    hid = wg.shape[1]
    rows = ex * tl
    half = n // tn
    cap = slot_ref.shape[1]
    chunks = a2s.shape[0]
    per = n // chunks

    def remote(s, r, ssem, rsem, dd, ee, tt):
        return pltpu.make_async_remote_copy(
            src_ref=s, dst_ref=r, send_sem=ssem, recv_sem=rsem,
            device_id=(dd, ee, tt), device_id_type=MESH,
        )

    rows_in = [
        pltpu.make_async_copy(x_hbm, x_ref, t_sem.at[0]),
        pltpu.make_async_copy(dy_hbm, dy_ref, t_sem.at[1]),
    ]
    for load in rows_in:
        load.start()
    barrier = pltpu.get_barrier_semaphore()
    greeted = 0
    for dd in range(n):
        for ee in range(ex):
            for tt in range(tn):
                if (dd and ee) or not (dd or ee or tt):
                    continue
                pl.semaphore_signal(
                    barrier, inc=1,
                    device_id=(lax.rem(d + dd, n), lax.rem(e + ee, ex), lax.rem(t + tt, tn)),
                    device_id_type=MESH,
                )
                greeted += 1

    loads = [
        pltpu.make_async_copy(wg_hbm.at[0], wg, w_sem.at[0]),
        pltpu.make_async_copy(wu_hbm.at[0], wu, w_sem.at[1]),
        pltpu.make_async_copy(wd_hbm.at[0], wd, w_sem.at[2]),
    ]
    for load in loads:
        load.start()

    for load in rows_in:
        load.wait()
    for b in range(n):
        cols = slice(b * bw, (b + 1) * bw)
        both = jnp.concatenate([x_ref[:, cols].astype(F32), dy_ref[:, cols].astype(F32)], axis=0)
        src[b] = both.astype(BF16)
    full[d, e] = src[d]
    gsend[...] = jnp.zeros_like(gsend)

    pl.semaphore_wait(barrier, greeted)

    to_dp = []
    for k in range(1, n):
        p = lax.rem(d + k, n)
        c = remote(src.at[p], full.at[d, e], a1s.at[p], a1r.at[d], p, e, t)
        c.start()
        to_dp.append(c)
    to_expert = []
    to_owner = []
    work = ((xs, wg, nn), (xs, wu, nn), (ys, wd, nt))

    def send_product(i, g):
        return remote(ps.at[i, g], pr.at[i, d], bs.at[i, g], br.at[i, d], g, e, t)

    for step in range(chunks + 1):
        if step < chunks:
            chunk = lax.rem(d // per + step, chunks)
            for q in range(per):
                g = chunk * per + q
                if per == 1:
                    if step:
                        remote(src.at[g], full.at[g, e], a1s.at[g], a1r.at[g], g, e, t).wait_recv()
                else:
                    @pl.when(g != d)
                    def _():
                        remote(src.at[g], full.at[g, e], a1s.at[g], a1r.at[g], g, e, t).wait_recv()
            span = pl.ds(chunk * per, per)
            for j in range(1, ex):
                p = lax.rem(e + j, ex)
                c = remote(full.at[span, e], full.at[span, e], a2s.at[chunk, p], a2r.at[chunk, e], d, p, t)
                c.start()
                to_expert.append(c)
        if step:
            chunk = lax.rem(d // per + step - 1, chunks)
            span = pl.ds(chunk * per, per)
            for j in range(1, ex):
                p = lax.rem(e + j, ex)
                remote(full.at[span, p], full.at[span, p], a2s.at[chunk, p], a2r.at[chunk, p], d, p, t).wait_recv()
            place = pl.ds(pl.multiple_of(chunk * (per * rows), per * rows), per * rows)
            wide = full[span].astype(F32)
            xs[place, :] = wide[:, :, :tl].reshape(per * rows, bw).astype(BF16)
            ys[place, :] = wide[:, :, tl:].reshape(per * rows, bw).astype(BF16)
            for i, (act, w, mul) in enumerate(work):
                if step == 1:
                    loads[i].wait()
                ps[i, span] = mul(act[place, :], w[...]).astype(BF16).reshape(per, rows, hid)
                for q in range(per):
                    g = chunk * per + q
                    if per == 1:
                        if step > 1:
                            c = send_product(i, g)
                            c.start()
                            to_owner.append(c)
                    else:
                        @pl.when(g != d)
                        def _():
                            send_product(i, g).start()
    for c in to_dp:
        c.wait_send()
    for c in to_expert:
        c.wait_send()
    xt[...] = xs[...].T

    iota_slot = lax.broadcasted_iota(jnp.int32, (1, cap), 1)
    live = iota_slot < count_ref[0]
    gate_live = jnp.where(live, gate_ref[...], 0.0)
    holds = lax.broadcasted_iota(jnp.int32, (rows, cap), 0) == slot_ref[...]
    gate_tok = jnp.sum(jnp.where(holds, gate_live, 0.0), axis=1, keepdims=True)

    sums = []
    for i in range(3):
        total = ps[i, d].astype(F32)
        for k in range(1, n):
            p = lax.rem(d + k, n)
            remote(ps.at[i, p], pr.at[i, p], bs.at[i, p], br.at[i, p], p, e, t).wait_recv()
            total = total + pr[i, p].astype(F32)
        sums.append(total)
    pre_gate, pre_up, back = sums
    sig = 1.0 / (1.0 + jnp.exp(-pre_gate))
    silu = pre_gate * sig
    hidden = silu * pre_up
    d_hidden = gate_tok * back
    dgu[d, 0] = (d_hidden * pre_up * (sig * (1.0 + pre_gate * (1.0 - sig)))).astype(BF16)
    dgu[d, 1] = (d_hidden * silu).astype(BF16)
    to_all = []
    for k in range(1, n):
        p = lax.rem(d + k, n)
        c = remote(dgu.at[d], dgu.at[d], cs.at[p], cr.at[d], p, e, t)
        c.start()
        to_all.append(c)
    dsc[d] = (gate_tok * hidden).astype(BF16)
    terms = jnp.sum(hidden * back, axis=1, keepdims=True)
    gsend[0:1, 0:cap] = jnp.where(
        live, jnp.sum(jnp.where(holds, terms, 0.0), axis=0, keepdims=True), 0.0
    )
    for k in range(1, tn):
        p = lax.rem(t + k, tn)
        c = remote(gsend, grecv.at[t], gs.at[p], gr.at[t], d, e, p)
        c.start()
        to_all.append(c)

    for k in range(1, n):
        p = lax.rem(d + k, n)
        remote(dgu.at[p], dgu.at[p], cs.at[p], cr.at[p], p, e, t).wait_recv()
    for k in range(1, n):
        p = lax.rem(d + k, n)
        c = remote(dsc.at[d], dsc.at[d], ss.at[p], sr.at[d], p, e, t)
        c.start()
        to_all.append(c)
    all_gate = dgu[:, 0].reshape(n * rows, hid)
    all_up = dgu[:, 1].reshape(n * rows, hid)
    d_rows = (nt(all_gate, wg[...]) + nt(all_up, wu[...])).reshape(n, ex, tl, bw)
    for ee in range(ex):
        for tt in range(tn):
            part = d_rows[tt * half:(tt + 1) * half, ee].reshape(half * tl, bw)
            dsend[ee * tn + tt] = part.astype(BF16)
    me = e * tn + t
    for ee in range(ex):
        for tt in range(tn):
            if ee or tt:
                pe, pt = lax.rem(e + ee, ex), lax.rem(t + tt, tn)
                c = remote(dsend.at[pe * tn + pt], drecv.at[me], ds_.at[pe * tn + pt], dr.at[me], d, pe, pt)
                c.start()
                to_all.append(c)

    ag_ref[...] = all_gate
    au_ref[...] = all_up

    total = dsend[me].astype(F32)
    for ee in range(ex):
        for tt in range(tn):
            if ee or tt:
                other = lax.rem(e + ee, ex) * tn + lax.rem(t + tt, tn)
                remote(dsend.at[other], drecv.at[other], ds_.at[other], dr.at[other], d, e, t).wait_recv()
                total = total + drecv[other].astype(F32)
    mine = d // half == t
    for q in range(half):
        part = total[q * tl:(q + 1) * tl]
        esend[q] = jnp.concatenate([part[:, :bw // 2], part[:, bw // 2:]], axis=0).astype(BF16)
        g = t * half + q
        for tt in range(tn):
            here = jnp.logical_and(g == d, t == tt)

            @pl.when(jnp.logical_not(here))
            def _():
                remote(esend.at[q], erecv.at[d], es.at[q, tt], er.at[d], g, e, tt).start()

            @pl.when(here)
            def _():
                erecv[d] = esend[q]

    for k in range(1, n):
        p = lax.rem(d + k, n)
        remote(dsc.at[p], dsc.at[p], ss.at[p], sr.at[p], p, e, t).wait_recv()
    st_ref[...] = dsc[...].reshape(n * rows, hid).T

    gate_sum = gsend[0:1, 0:cap]
    for k in range(1, tn):
        p = lax.rem(t + k, tn)
        remote(gsend, grecv.at[p], gs.at[p], gr.at[p], d, e, p).wait_recv()
        gate_sum = gate_sum + grecv[p, 0:1, 0:cap]
    gg_ref[...] = gate_sum

    for s in range(n):
        @pl.when(jnp.logical_not(jnp.logical_and(s == d, mine)))
        def _():
            remote(esend.at[0], erecv.at[s], es.at[0, 0], er.at[s], d, e, t).wait_recv()
        wide = erecv[s].astype(F32)
        gt_ref[:, s * bw:s * bw + bw // 2] = wide[:tl].astype(BF16)
        gt_ref[:, s * bw + bw // 2:(s + 1) * bw] = wide[tl:].astype(BF16)

    if per > 1:
        for i in range(3):
            for k in range(1, n):
                send_product(i, lax.rem(d + k, n)).wait_send()
    for c in to_owner + to_all:
        c.wait_send()
    for q in range(half):
        for tt in range(tn):
            @pl.when(jnp.logical_not(jnp.logical_and(t * half + q == d, t == tt)))
            def _():
                remote(esend.at[q], erecv.at[d], es.at[q, tt], er.at[d], d, e, tt).wait_send()


def weight_grads(
    gt_in, gg_in, xt, ys, ag, au, st, gt_hbm, gg_hbm, gwg_hbm, gwu_hbm, gwd_hbm, owg, owu, owd, sem
):
    copies = [
        pltpu.make_async_copy(gt_in, gt_hbm, sem.at[0]),
        pltpu.make_async_copy(gg_in, gg_hbm, sem.at[1]),
    ]
    for c in copies:
        c.start()
    work = ((xt, ag, owg, gwg_hbm), (xt, au, owu, gwu_hbm), (st, ys, owd, gwd_hbm))
    for i, (left, right, held, out) in enumerate(work):
        tall = left.shape[0]
        piece = tall // 2
        for j in range(2):
            span = slice(j * piece, (j + 1) * piece)
            held[span, :] = nn(left[span, :], right[...]).astype(BF16)
            c = pltpu.make_async_copy(
                held.at[span], out.at[0, span], sem.at[2 + 2 * i + j]
            )
            c.start()
            copies.append(c)
    for c in copies:
        c.wait()


def shards(n, ex, tn, tokens, grad_out, slot_token, slot_count, slot_gate, w_gate, w_up, w_down):
    tl, width = tokens.shape
    bw, hid = w_gate.shape[1:]
    rows = ex * tl
    all_rows = n * rows
    half = n // tn
    chunks = min(n, 4)
    vmem = pl.BlockSpec(memory_space=pltpu.VMEM)
    hbm = pl.BlockSpec(memory_space=pltpu.HBM)
    outs = (
        jax.ShapeDtypeStruct((tl, width), BF16),
        jax.ShapeDtypeStruct(slot_gate.shape, F32),
        jax.ShapeDtypeStruct(w_gate.shape, BF16),
        jax.ShapeDtypeStruct(w_up.shape, BF16),
        jax.ShapeDtypeStruct(w_down.shape, BF16),
    )
    dma = pltpu.SemaphoreType.DMA
    results = pl.pallas_call(
        functools.partial(kernel, n, ex, tn),
        out_shape=outs[:2] + (
            jax.ShapeDtypeStruct((bw, all_rows), BF16),
            jax.ShapeDtypeStruct((all_rows, bw), BF16),
            jax.ShapeDtypeStruct((all_rows, hid), BF16),
            jax.ShapeDtypeStruct((all_rows, hid), BF16),
            jax.ShapeDtypeStruct((hid, all_rows), BF16),
        ),
        in_specs=[hbm, hbm, vmem, pl.BlockSpec(memory_space=pltpu.SMEM), vmem]
        + [hbm] * 3,
        out_specs=(vmem,) * 7,
        scratch_shapes=[
            pltpu.VMEM((tl, width), BF16),
            pltpu.VMEM((tl, width), BF16),
            pltpu.VMEM((bw, hid), BF16),
            pltpu.VMEM((bw, hid), BF16),
            pltpu.VMEM((hid, bw), BF16),
            pltpu.VMEM((n, 2 * tl, bw), BF16),
            pltpu.VMEM((n, ex, 2 * tl, bw), BF16),
            pltpu.VMEM((all_rows, bw), BF16),
            pltpu.VMEM((3, n, rows, hid), BF16),
            pltpu.VMEM((3, n, rows, hid), BF16),
            pltpu.VMEM((n, 2, rows, hid), BF16),
            pltpu.VMEM((n, rows, hid), BF16),
            pltpu.VMEM((ex * tn, half * tl, bw), BF16),
            pltpu.VMEM((ex * tn, half * tl, bw), BF16),
            pltpu.VMEM((half, 2 * tl, bw // 2), BF16),
            pltpu.VMEM((n, 2 * tl, bw // 2), BF16),
            pltpu.VMEM((8, 128), F32),
            pltpu.VMEM((tn, 8, 128), F32),
            dma((2,)), dma((3,)),
            dma((n,)), dma((n,)),
            dma((chunks, ex)), dma((chunks, ex)),
            dma((3, n)), dma((3, n)),
            dma((n,)), dma((n,)),
            dma((n,)), dma((n,)),
            dma((ex * tn,)), dma((ex * tn,)),
            dma((half, tn)), dma((n,)),
            dma((tn,)), dma((tn,)),
        ],
        compiler_params=pltpu.CompilerParams(
            collective_id=0, has_side_effects=True, vmem_limit_bytes=64 * 1024 * 1024 - 65536
        ),
    )(tokens, grad_out, slot_token, slot_count, slot_gate, w_gate, w_up, w_down)
    return pl.pallas_call(
        weight_grads,
        out_shape=outs,
        in_specs=[vmem] * 7,
        out_specs=(hbm,) * 5,
        scratch_shapes=[
            pltpu.VMEM((bw, hid), BF16),
            pltpu.VMEM((bw, hid), BF16),
            pltpu.VMEM((hid, bw), BF16),
            dma((8,)),
        ],
        compiler_params=pltpu.CompilerParams(vmem_limit_bytes=64 * 1024 * 1024 - 65536),
    )(*results)


def solution(mesh):
    n, ex, tn = (mesh.shape[a] for a in ("dp", "expert", "tensor"))
    return jax.shard_map(
        functools.partial(shards, n, ex, tn),
        mesh=mesh,
        in_specs=(
            P(("dp", "expert"), None),
            P(("dp", "expert"), None),
            P(("dp", "expert"), None),
            P(("dp", "expert")),
            P(("dp", "expert"), None),
            P("expert", "dp", "tensor"),
            P("expert", "dp", "tensor"),
            P("expert", "tensor", "dp"),
        ),
        out_specs=(
            P(("dp", "expert"), None),
            P(("dp", "expert"), None),
            P("expert", "dp", "tensor"),
            P("expert", "dp", "tensor"),
            P("expert", "tensor", "dp"),
        ),
        check_vma=False,
    )
```

```python
import functools

import jax
import jax.numpy as jnp
from jax import lax
from jax.experimental import pallas as pl
from jax.experimental.pallas import tpu as pltpu
from jax.sharding import PartitionSpec as P

MESH = pl.DeviceIdType.MESH
F32 = jnp.float32
BF16 = jnp.bfloat16


def nn(a, b):
    return lax.dot_general(a, b, (((1,), (0,)), ((), ())), preferred_element_type=F32)


def nt(a, b):
    return lax.dot_general(a, b, (((1,), (1,)), ((), ())), preferred_element_type=F32)


def kernel(
    n, ex, tn,
    x_hbm, dy_hbm, slot_ref, count_ref, gate_ref, wg_hbm, wu_hbm, wd_hbm,
    gt_ref, gg_ref, xt, ys, ag_ref, au_ref, st_ref,
    x_ref, dy_ref, wg, wu, wd, src, full, xs, ps, pr, dgu, dsc,
    dsend, drecv, esend, erecv, gsend, grecv,
    t_sem, w_sem, a1s, a1r, a2s, a2r, bs, br, cs, cr, ss, sr, ds_, dr, es, er, gs, gr,
):
    d = lax.axis_index("dp")
    e = lax.axis_index("expert")
    t = lax.axis_index("tensor")
    tl = x_ref.shape[0]
    bw = xs.shape[1]
    hid = wg.shape[1]
    rows = ex * tl
    half = n // tn
    cap = slot_ref.shape[1]
    chunks = a2s.shape[0]
    per = n // chunks

    def remote(s, r, ssem, rsem, dd, ee, tt):
        return pltpu.make_async_remote_copy(
            src_ref=s, dst_ref=r, send_sem=ssem, recv_sem=rsem,
            device_id=(dd, ee, tt), device_id_type=MESH,
        )

    rows_in = [
        pltpu.make_async_copy(x_hbm, x_ref, t_sem.at[0]),
        pltpu.make_async_copy(dy_hbm, dy_ref, t_sem.at[1]),
    ]
    for load in rows_in:
        load.start()
    barrier = pltpu.get_barrier_semaphore()
    greeted = 0
    for dd in range(n):
        for ee in range(ex):
            for tt in range(tn):
                if (dd and ee) or not (dd or ee or tt):
                    continue
                pl.semaphore_signal(
                    barrier, inc=1,
                    device_id=(lax.rem(d + dd, n), lax.rem(e + ee, ex), lax.rem(t + tt, tn)),
                    device_id_type=MESH,
                )
                greeted += 1

    loads = [
        pltpu.make_async_copy(wg_hbm.at[0], wg, w_sem.at[0]),
        pltpu.make_async_copy(wu_hbm.at[0], wu, w_sem.at[1]),
        pltpu.make_async_copy(wd_hbm.at[0], wd, w_sem.at[2]),
    ]
    for load in loads:
        load.start()

    for load in rows_in:
        load.wait()
    for b in range(n):
        cols = slice(b * bw, (b + 1) * bw)
        both = jnp.concatenate([x_ref[:, cols].astype(F32), dy_ref[:, cols].astype(F32)], axis=0)
        src[b] = both.astype(BF16)
    full[d, e] = src[d]
    gsend[...] = jnp.zeros_like(gsend)

    pl.semaphore_wait(barrier, greeted)

    to_dp = []
    for k in reversed(range(1, n)):
        p = lax.rem(d + k, n)
        c = remote(src.at[p], full.at[d, e], a1s.at[p], a1r.at[d], p, e, t)
        c.start()
        to_dp.append(c)
    to_expert = []
    to_owner = []
    work = ((xs, wg, nn), (xs, wu, nn), (ys, wd, nt))

    def send_product(i, g):
        return remote(ps.at[i, g], pr.at[i, d], bs.at[i, g], br.at[i, d], g, e, t)

    for step in range(chunks + 1):
        if step < chunks:
            chunk = lax.rem(d // per + step, chunks)
            for q in range(per):
                g = chunk * per + q
                if per == 1:
                    if step:
                        remote(src.at[g], full.at[g, e], a1s.at[g], a1r.at[g], g, e, t).wait_recv()
                else:
                    @pl.when(g != d)
                    def _():
                        remote(src.at[g], full.at[g, e], a1s.at[g], a1r.at[g], g, e, t).wait_recv()
            span = pl.ds(chunk * per, per)
            for j in range(1, ex):
                p = lax.rem(e + j, ex)
                c = remote(full.at[span, e], full.at[span, e], a2s.at[chunk, p], a2r.at[chunk, e], d, p, t)
                c.start()
                to_expert.append(c)
        if step:
            chunk = lax.rem(d // per + step - 1, chunks)
            span = pl.ds(chunk * per, per)
            for j in range(1, ex):
                p = lax.rem(e + j, ex)
                remote(full.at[span, p], full.at[span, p], a2s.at[chunk, p], a2r.at[chunk, p], d, p, t).wait_recv()
            place = pl.ds(pl.multiple_of(chunk * (per * rows), per * rows), per * rows)
            wide = full[span].astype(F32)
            xs[place, :] = wide[:, :, :tl].reshape(per * rows, bw).astype(BF16)
            ys[place, :] = wide[:, :, tl:].reshape(per * rows, bw).astype(BF16)
            for i, (act, w, mul) in enumerate(work):
                if step == 1:
                    loads[i].wait()
                ps[i, span] = mul(act[place, :], w[...]).astype(BF16).reshape(per, rows, hid)
                for q in range(per):
                    g = chunk * per + q
                    if per == 1:
                        if step > 1:
                            c = send_product(i, g)
                            c.start()
                            to_owner.append(c)
                    else:
                        @pl.when(g != d)
                        def _():
                            send_product(i, g).start()
    for c in to_dp:
        c.wait_send()
    for c in to_expert:
        c.wait_send()
    xt[...] = xs[...].T

    iota_slot = lax.broadcasted_iota(jnp.int32, (1, cap), 1)
    live = iota_slot < count_ref[0]
    gate_live = jnp.where(live, gate_ref[...], 0.0)
    holds = lax.broadcasted_iota(jnp.int32, (rows, cap), 0) == slot_ref[...]
    gate_tok = jnp.sum(jnp.where(holds, gate_live, 0.0), axis=1, keepdims=True)

    sums = []
    for i in range(3):
        total = ps[i, d].astype(F32)
        for k in range(1, n):
            p = lax.rem(d + k, n)
            remote(ps.at[i, p], pr.at[i, p], bs.at[i, p], br.at[i, p], p, e, t).wait_recv()
            total = total + pr[i, p].astype(F32)
        sums.append(total)
    pre_gate, pre_up, back = sums
    sig = 1.0 / (1.0 + jnp.exp(-pre_gate))
    silu = pre_gate * sig
    hidden = silu * pre_up
    d_hidden = gate_tok * back
    dgu[d, 0] = (d_hidden * pre_up * (sig * (1.0 + pre_gate * (1.0 - sig)))).astype(BF16)
    dgu[d, 1] = (d_hidden * silu).astype(BF16)
    to_all = []
    for k in range(1, n):
        p = lax.rem(d + k, n)
        c = remote(dgu.at[d], dgu.at[d], cs.at[p], cr.at[d], p, e, t)
        c.start()
        to_all.append(c)
    dsc[d] = (gate_tok * hidden).astype(BF16)
    terms = jnp.sum(hidden * back, axis=1, keepdims=True)
    gsend[0:1, 0:cap] = jnp.where(
        live, jnp.sum(jnp.where(holds, terms, 0.0), axis=0, keepdims=True), 0.0
    )
    for k in range(1, tn):
        p = lax.rem(t + k, tn)
        c = remote(gsend, grecv.at[t], gs.at[p], gr.at[t], d, e, p)
        c.start()
        to_all.append(c)

    for k in range(1, n):
        p = lax.rem(d + k, n)
        remote(dgu.at[p], dgu.at[p], cs.at[p], cr.at[p], p, e, t).wait_recv()
    for k in range(1, n):
        p = lax.rem(d + k, n)
        c = remote(dsc.at[d], dsc.at[d], ss.at[p], sr.at[d], p, e, t)
        c.start()
        to_all.append(c)
    all_gate = dgu[:, 0].reshape(n * rows, hid)
    all_up = dgu[:, 1].reshape(n * rows, hid)
    d_rows = (nt(all_gate, wg[...]) + nt(all_up, wu[...])).reshape(n, ex, tl, bw)
    for ee in range(ex):
        for tt in range(tn):
            part = d_rows[tt * half:(tt + 1) * half, ee].reshape(half * tl, bw)
            dsend[ee * tn + tt] = part.astype(BF16)
    me = e * tn + t
    for ee in range(ex):
        for tt in range(tn):
            if ee or tt:
                pe, pt = lax.rem(e + ee, ex), lax.rem(t + tt, tn)
                c = remote(dsend.at[pe * tn + pt], drecv.at[me], ds_.at[pe * tn + pt], dr.at[me], d, pe, pt)
                c.start()
                to_all.append(c)

    ag_ref[...] = all_gate
    au_ref[...] = all_up

    total = dsend[me].astype(F32)
    for ee in range(ex):
        for tt in range(tn):
            if ee or tt:
                other = lax.rem(e + ee, ex) * tn + lax.rem(t + tt, tn)
                remote(dsend.at[other], drecv.at[other], ds_.at[other], dr.at[other], d, e, t).wait_recv()
                total = total + drecv[other].astype(F32)
    mine = d // half == t
    for q in range(half):
        part = total[q * tl:(q + 1) * tl]
        esend[q] = jnp.concatenate([part[:, :bw // 2], part[:, bw // 2:]], axis=0).astype(BF16)
        g = t * half + q
        for tt in range(tn):
            here = jnp.logical_and(g == d, t == tt)

            @pl.when(jnp.logical_not(here))
            def _():
                remote(esend.at[q], erecv.at[d], es.at[q, tt], er.at[d], g, e, tt).start()

            @pl.when(here)
            def _():
                erecv[d] = esend[q]

    for k in range(1, n):
        p = lax.rem(d + k, n)
        remote(dsc.at[p], dsc.at[p], ss.at[p], sr.at[p], p, e, t).wait_recv()
    st_ref[...] = dsc[...].reshape(n * rows, hid).T

    gate_sum = gsend[0:1, 0:cap]
    for k in range(1, tn):
        p = lax.rem(t + k, tn)
        remote(gsend, grecv.at[p], gs.at[p], gr.at[p], d, e, p).wait_recv()
        gate_sum = gate_sum + grecv[p, 0:1, 0:cap]
    gg_ref[...] = gate_sum

    for s in range(n):
        @pl.when(jnp.logical_not(jnp.logical_and(s == d, mine)))
        def _():
            remote(esend.at[0], erecv.at[s], es.at[0, 0], er.at[s], d, e, t).wait_recv()
        wide = erecv[s].astype(F32)
        gt_ref[:, s * bw:s * bw + bw // 2] = wide[:tl].astype(BF16)
        gt_ref[:, s * bw + bw // 2:(s + 1) * bw] = wide[tl:].astype(BF16)

    if per > 1:
        for i in range(3):
            for k in range(1, n):
                send_product(i, lax.rem(d + k, n)).wait_send()
    for c in to_owner + to_all:
        c.wait_send()
    for q in range(half):
        for tt in range(tn):
            @pl.when(jnp.logical_not(jnp.logical_and(t * half + q == d, t == tt)))
            def _():
                remote(esend.at[q], erecv.at[d], es.at[q, tt], er.at[d], d, e, tt).wait_send()


def weight_grads(
    gt_in, gg_in, xt, ys, ag, au, st, gt_hbm, gg_hbm, gwg_hbm, gwu_hbm, gwd_hbm, owg, owu, owd, sem
):
    copies = [
        pltpu.make_async_copy(gt_in, gt_hbm, sem.at[0]),
        pltpu.make_async_copy(gg_in, gg_hbm, sem.at[1]),
    ]
    for c in copies:
        c.start()
    work = ((xt, ag, owg, gwg_hbm), (xt, au, owu, gwu_hbm), (st, ys, owd, gwd_hbm))
    for i, (left, right, held, out) in enumerate(work):
        tall = left.shape[0]
        piece = tall // 2
        for j in range(2):
            span = slice(j * piece, (j + 1) * piece)
            held[span, :] = nn(left[span, :], right[...]).astype(BF16)
            c = pltpu.make_async_copy(
                held.at[span], out.at[0, span], sem.at[2 + 2 * i + j]
            )
            c.start()
            copies.append(c)
    for c in copies:
        c.wait()


def shards(n, ex, tn, tokens, grad_out, slot_token, slot_count, slot_gate, w_gate, w_up, w_down):
    tl, width = tokens.shape
    bw, hid = w_gate.shape[1:]
    rows = ex * tl
    all_rows = n * rows
    half = n // tn
    chunks = min(n, 4)
    vmem = pl.BlockSpec(memory_space=pltpu.VMEM)
    hbm = pl.BlockSpec(memory_space=pltpu.HBM)
    outs = (
        jax.ShapeDtypeStruct((tl, width), BF16),
        jax.ShapeDtypeStruct(slot_gate.shape, F32),
        jax.ShapeDtypeStruct(w_gate.shape, BF16),
        jax.ShapeDtypeStruct(w_up.shape, BF16),
        jax.ShapeDtypeStruct(w_down.shape, BF16),
    )
    dma = pltpu.SemaphoreType.DMA
    results = pl.pallas_call(
        functools.partial(kernel, n, ex, tn),
        out_shape=outs[:2] + (
            jax.ShapeDtypeStruct((bw, all_rows), BF16),
            jax.ShapeDtypeStruct((all_rows, bw), BF16),
            jax.ShapeDtypeStruct((all_rows, hid), BF16),
            jax.ShapeDtypeStruct((all_rows, hid), BF16),
            jax.ShapeDtypeStruct((hid, all_rows), BF16),
        ),
        in_specs=[hbm, hbm, vmem, pl.BlockSpec(memory_space=pltpu.SMEM), vmem]
        + [hbm] * 3,
        out_specs=(vmem,) * 7,
        scratch_shapes=[
            pltpu.VMEM((tl, width), BF16),
            pltpu.VMEM((tl, width), BF16),
            pltpu.VMEM((bw, hid), BF16),
            pltpu.VMEM((bw, hid), BF16),
            pltpu.VMEM((hid, bw), BF16),
            pltpu.VMEM((n, 2 * tl, bw), BF16),
            pltpu.VMEM((n, ex, 2 * tl, bw), BF16),
            pltpu.VMEM((all_rows, bw), BF16),
            pltpu.VMEM((3, n, rows, hid), BF16),
            pltpu.VMEM((3, n, rows, hid), BF16),
            pltpu.VMEM((n, 2, rows, hid), BF16),
            pltpu.VMEM((n, rows, hid), BF16),
            pltpu.VMEM((ex * tn, half * tl, bw), BF16),
            pltpu.VMEM((ex * tn, half * tl, bw), BF16),
            pltpu.VMEM((half, 2 * tl, bw // 2), BF16),
            pltpu.VMEM((n, 2 * tl, bw // 2), BF16),
            pltpu.VMEM((8, 128), F32),
            pltpu.VMEM((tn, 8, 128), F32),
            dma((2,)), dma((3,)),
            dma((n,)), dma((n,)),
            dma((chunks, ex)), dma((chunks, ex)),
            dma((3, n)), dma((3, n)),
            dma((n,)), dma((n,)),
            dma((n,)), dma((n,)),
            dma((ex * tn,)), dma((ex * tn,)),
            dma((half, tn)), dma((n,)),
            dma((tn,)), dma((tn,)),
        ],
        compiler_params=pltpu.CompilerParams(
            collective_id=0, has_side_effects=True, vmem_limit_bytes=64 * 1024 * 1024 - 65536
        ),
    )(tokens, grad_out, slot_token, slot_count, slot_gate, w_gate, w_up, w_down)
    return pl.pallas_call(
        weight_grads,
        out_shape=outs,
        in_specs=[vmem] * 7,
        out_specs=(hbm,) * 5,
        scratch_shapes=[
            pltpu.VMEM((bw, hid), BF16),
            pltpu.VMEM((bw, hid), BF16),
            pltpu.VMEM((hid, bw), BF16),
            dma((8,)),
        ],
        compiler_params=pltpu.CompilerParams(vmem_limit_bytes=64 * 1024 * 1024 - 65536),
    )(*results)


def solution(mesh):
    n, ex, tn = (mesh.shape[a] for a in ("dp", "expert", "tensor"))
    return jax.shard_map(
        functools.partial(shards, n, ex, tn),
        mesh=mesh,
        in_specs=(
            P(("dp", "expert"), None),
            P(("dp", "expert"), None),
            P(("dp", "expert"), None),
            P(("dp", "expert")),
            P(("dp", "expert"), None),
            P("expert", "dp", "tensor"),
            P("expert", "dp", "tensor"),
            P("expert", "tensor", "dp"),
        ),
        out_specs=(
            P(("dp", "expert"), None),
            P(("dp", "expert"), None),
            P("expert", "dp", "tensor"),
            P("expert", "dp", "tensor"),
            P("expert", "tensor", "dp"),
        ),
        check_vma=False,
    )
```
